32 devices in a mesh: fsdp: 8 (over z, y), seq: 4 (over x, core).
Axes of the slice: x: 2, y: 2, z: 4, core: 2. Of those that a mesh axis runs over, the one named last changes fastest.
Arguments:
- tokens: bfloat16 [8, 512, 8192], P('fsdp', 'seq'), may hold values from -6 to 6
- queries: bfloat16 [8, 512, 8192], P('fsdp', None, 'seq'), may hold values from -6 to 6
- key_weight: bfloat16 [8192, 1024], P('fsdp', 'seq'), may hold values from -1 to 1
- u_factor: float32 [8192, 64], P('fsdp'), may hold values from -6 to 6
- v_factor: float32 [1024, 64], replicated, may hold values from -6 to 6
Outputs:
- update: float32 [8192, 1024], P('fsdp')
- losses: float32 [2], replicated
The draws below stay inside these ranges and needn't reach their ends.
All inputs are finite; a program needn't handle non-finite values.
Results may differ from the reference program's by a relative error of at most 0.0003.
Values may be sent and summed in bfloat16 or wider, within the bound.
A program may use at most 64 MiB of HBM per device.

```python
import math
import jax
import jax.numpy as jnp
from jax import lax

D = 8192
HQ = 64
KVH = 8
HD = 128
R = 64
KD = 1024
GROUP = 8
LENGTH = 512
SEQS = 8


def common_weight(key):
    weight_key = jax.random.fold_in(key, 101)
    values = jax.random.normal(weight_key, (D, KD), jnp.float32)
    return jnp.clip(values * (1.0 / math.sqrt(D)), -1.0, 1.0)


def sequence_scales(low, ratio):
    steps = jnp.arange(SEQS).astype(jnp.float32) / float(max(SEQS - 1, 1))
    return low * jnp.exp(steps * math.log(ratio))


def draw_key_weight(key, part):
    return common_weight(key).astype(jnp.bfloat16)


def draw_tokens(key, part):
    token_key = jax.random.fold_in(key, 303)
    values = jnp.clip(jax.random.normal(token_key, (SEQS, LENGTH, D), jnp.float32), -6.0, 6.0)
    return values.astype(jnp.bfloat16)


def draw_queries(key, part):
    query_key = jax.random.fold_in(key, 404)
    values = jax.random.normal(query_key, (SEQS, LENGTH, HQ * HD), jnp.float32)
    values = jnp.clip(values * sequence_scales(0.4, 8.0)[:, None, None], -6.0, 6.0)
    return values.astype(jnp.bfloat16)


def steps_of(rng, extent, shards, least, high):
    loudness, own = 1.0, jax.random.fold_in(rng, 6)
    for axis_at, parts in shards:
        steps = jnp.exp(jax.random.uniform(jax.random.fold_in(own, axis_at), (parts,), jnp.float32, least / len(shards), high / len(shards)))
        loudness = loudness * jnp.repeat(steps, extent[axis_at] // parts).reshape([-1 if axis == axis_at else 1 for axis in range(len(extent))])
    return loudness


def noise(key, shape, width, bound, shards=(), kind=jnp.bfloat16):
    values = jax.random.normal(key, shape, jnp.float32) * width
    if len(shards) > 0:
        values = steps_of(key, shape, shards, -0.22, 0.18) * values
    return jnp.clip(values, min=-bound, max=bound).astype(kind)


def setup_inputs(seed: int = 0) -> dict:
    seeds = jax.random.split(jax.random.key(seed), 6)
    tokens = draw_tokens(jax.random.fold_in(seeds[5], 71), 0)
    queries = draw_queries(jax.random.fold_in(seeds[5], 71), 0)
    key_weight = draw_key_weight(jax.random.fold_in(seeds[5], 71), 0)
    u_factor = noise(seeds[3], (D, R), 1.0, 6.0, ((0, 8),), jnp.float32)
    v_factor = noise(seeds[4], (KD, R), 1.0, 6.0, (), jnp.float32)
    return {"tokens": tokens, "queries": queries, "key_weight": key_weight, "u_factor": u_factor, "v_factor": v_factor}


def orthonormal(factor):
    for turn in range(2):
        gram = jnp.dot(factor.T.astype(jnp.float32), factor.astype(jnp.float32), precision=lax.Precision.HIGHEST, preferred_element_type=jnp.float32)
        lower = jnp.linalg.cholesky(gram)
        factor = lax.linalg.triangular_solve(lower, factor, left_side=False, lower=True, transpose_a=True)
    return factor

def log_partition(query_rows, keys):
    length = query_rows.shape[0]
    heads = query_rows.astype(jnp.float32).reshape(length, KVH, GROUP, HD)
    key_heads = keys.astype(jnp.float32).reshape(2, length, KVH, HD)
    scores = jnp.einsum('tkgd,npkd->nkgtp', heads, key_heads) * (1.0 / math.sqrt(HD))
    places = jnp.arange(length)
    causal = places[:, None] >= places[None, :]
    scores = jnp.where(causal, scores, -1e+30)
    top = lax.optimization_barrier(jnp.max(scores, axis=-1))
    total = lax.optimization_barrier(jnp.sum(jnp.where(causal, jnp.exp(scores - top[..., None]), 0.0), axis=-1))
    return lax.optimization_barrier(jnp.sum(top + jnp.log(total), axis=(1, 2, 3)))

def reference(tokens, queries, key_weight, u_factor, v_factor):
    q_u = orthonormal(u_factor)
    q_v = orthonormal(v_factor)
    q_low = q_u.astype(jnp.bfloat16)

    def one_sequence(pair):
        rows, query_rows = pair
        base = jnp.dot(rows.astype(jnp.float32), key_weight.astype(jnp.float32), preferred_element_type=jnp.float32)
        side = jnp.dot(rows.astype(jnp.float32), q_low.astype(jnp.float32), preferred_element_type=jnp.float32)
        offset = 2.0 * jnp.dot(side.astype(jnp.float32), q_v.T.astype(jnp.float32), precision=lax.Precision.HIGHEST, preferred_element_type=jnp.float32)
        keys = jnp.stack([base + offset, base - offset]).astype(jnp.bfloat16)
        return log_partition(query_rows, keys)
    sums = lax.optimization_barrier(jnp.sum(lax.map(one_sequence, (tokens, queries)), axis=0))
    losses = sums / (SEQS * LENGTH * HQ)
    unit = math.sqrt(D * KD / R)
    update = unit * jnp.dot(q_u.astype(jnp.float32), q_v.T.astype(jnp.float32), precision=lax.Precision.HIGHEST, preferred_element_type=jnp.float32)
    return (update, losses)
```

```python
import functools
import math

import jax
import jax.numpy as jnp
from jax import lax
from jax.experimental import pallas as pl
from jax.experimental.pallas import tpu as pltpu
from jax.sharding import PartitionSpec as P

D = 8192
HQ = 64
HD = 128
R = 64
KD = 1024
GROUP = 8
CHUNKS = 4
KT = 1024
BF = jnp.bfloat16
F32 = jnp.float32
MESH = pl.DeviceIdType.MESH
VMEM = pl.BlockSpec(memory_space=pltpu.VMEM)
ANY = pl.BlockSpec(memory_space=pl.ANY)


def dot(left, right, contract, precision=None):
    return lax.dot_general(left, right, ((contract[0], contract[1]), ((), ())), precision=precision, preferred_element_type=F32)


def exact(left, right, contract):
    return dot(left, right, contract, lax.Precision.HIGHEST)


def inverse_factors(grams):
    rows = lax.broadcasted_iota(jnp.int32, (R, 2 * R), 0)
    lanes = lax.broadcasted_iota(jnp.int32, (R, 2 * R), 1)
    unit = (lanes == rows + R).astype(F32)
    work = [jnp.concatenate([g, jnp.zeros((R, R), F32)], axis=1) + unit for g in grams]
    scales = [jnp.ones((R, 1), F32) for _ in grams]
    column_rows = lax.broadcasted_iota(jnp.int32, (R, 1), 0)
    for j in range(R):
        for n in range(len(work)):
            a = work[n]
            row = a[j : j + 1, :]
            column = a[:, j : j + 1]
            pivot = a[j : j + 1, j : j + 1]
            factor = jnp.where(column_rows > j, column * (1.0 / pivot), 0.0)
            scales[n] = jnp.where(column_rows == j, pivot, scales[n])
            work[n] = a - factor * row
    return [(a * lax.rsqrt(s))[:, R:] for a, s in zip(work, scales)]


def keys_kernel(nf, ns, x_hbm, w_hbm, u_ref, v_ref, keys_ref, qu_ref, qv_ref, xs, ws, qp, ql, gm, acc, sacc,
                in_sem, g_send, g_recv, q_send, q_recv, up_send, up_recv, dn_send, dn_recv, p_send, p_recv,
                b_send, b_recv, n_send, n_recv, r_send, r_recv):
    f = lax.axis_index("fsdp")
    s = lax.axis_index("seq")
    line = nf // 2
    a, b = f // 2, lax.rem(f, 2)
    mate = 2 * a + (1 - b)
    core = lax.rem(s, 2)
    brother = s - core + (1 - core)
    across = lax.rem(s + 2, ns)
    rows = u_ref.shape[0]
    half = rows // 2
    plen = xs.shape[0] // ns
    width = D // CHUNKS
    cols = ws.shape[1]

    load_x = pltpu.make_async_copy(x_hbm.at[0], xs.at[pl.ds(pl.multiple_of(s * plen, plen), plen), :], in_sem.at[0])
    load_w = pltpu.make_async_copy(w_hbm, ws.at[pl.ds(pl.multiple_of(f * rows, rows), rows), :], in_sem.at[1])
    load_x.start()
    load_w.start()

    barrier = pltpu.get_barrier_semaphore()

    @pl.loop(1, nf)
    def _(d):
        pl.semaphore_signal(barrier, inc=1, device_id=(lax.rem(f + d, nf), s), device_id_type=MESH)

    @pl.loop(1, ns)
    def _(d):
        pl.semaphore_signal(barrier, inc=1, device_id=(f, lax.rem(s + d, ns)), device_id_type=MESH)

    gram_v = exact(v_ref[...], v_ref[...], ((0,), (0,)))
    gram_u = exact(u_ref[...], u_ref[...], ((0,), (0,)))
    pl.semaphore_wait(barrier, nf - 1 + ns - 1)

    def gram_copy(turn, d):
        return pltpu.make_async_remote_copy(
            src_ref=gm.at[turn, f], dst_ref=gm.at[turn, f], send_sem=g_send.at[turn, d], recv_sem=g_recv.at[turn, d],
            device_id=(lax.rem(f + d, nf), s), device_id_type=MESH)

    def gram_arrival(turn, d):
        source = lax.rem(f + nf - d, nf)
        return pltpu.make_async_remote_copy(
            src_ref=gm.at[turn, source], dst_ref=gm.at[turn, source], send_sem=g_send.at[turn, d],
            recv_sem=g_recv.at[turn, d], device_id=(lax.rem(f + d, nf), s), device_id_type=MESH)

    def send_gram(turn, gram):
        gm[turn, f] = gram

        @pl.loop(1, nf)
        def _(d):
            gram_copy(turn, d).start()

    def sum_gram(turn):
        @pl.loop(1, nf)
        def _(d):
            gram_arrival(turn, d).wait_recv()

        return jnp.sum(gm[turn], axis=0)

    def block(index):
        return ws.at[pl.ds(pl.multiple_of(index * rows, rows), rows), :]

    def up(k):
        piece = block(2 * (a - k + 1) + b)
        return pltpu.make_async_remote_copy(src_ref=piece, dst_ref=piece, send_sem=up_send.at[k], recv_sem=up_recv.at[k],
                                            device_id=(f + 2, s), device_id_type=MESH)

    def down(k):
        piece = block(2 * (a + k - 1) + b)
        return pltpu.make_async_remote_copy(src_ref=piece, dst_ref=piece, send_sem=dn_send.at[k], recv_sem=dn_recv.at[k],
                                            device_id=(f - 2, s), device_id_type=MESH)

    def pair(at):
        piece = block(2 * at + b)
        return pltpu.make_async_remote_copy(src_ref=piece, dst_ref=piece, send_sem=p_send.at[at], recv_sem=p_recv.at[at],
                                            device_id=(mate, s), device_id_type=MESH)

    def pair_arrival(at):
        piece = block(2 * at + (1 - b))
        return pltpu.make_async_remote_copy(src_ref=piece, dst_ref=piece, send_sem=p_send.at[at], recv_sem=p_recv.at[at],
                                            device_id=(mate, s), device_id_type=MESH)

    def sends(k):
        @pl.when((a + 1 < line) & (a - k + 1 >= 0))
        def _():
            up(k).start()

        @pl.when((a > 0) & (a + k - 1 < line))
        def _():
            down(k).start()

    def relay(k):
        @pl.when(a - k >= 0)
        def _():
            piece = block(2 * (a - k) + b)
            pltpu.make_async_remote_copy(src_ref=piece, dst_ref=piece, send_sem=up_send.at[k], recv_sem=up_recv.at[k],
                                         device_id=(mate, s), device_id_type=MESH).wait_recv()

        @pl.when(a + k < line)
        def _():
            piece = block(2 * (a + k) + b)
            pltpu.make_async_remote_copy(src_ref=piece, dst_ref=piece, send_sem=dn_send.at[k], recv_sem=dn_recv.at[k],
                                         device_id=(mate, s), device_id_type=MESH).wait_recv()

        sends(k + 1)

        @pl.when(a - k >= 0)
        def _():
            pair(a - k).start()

        @pl.when(a + k < line)
        def _():
            pair(a + k).start()

    def tokens(owner, chunk):
        return xs.at[pl.ds(pl.multiple_of(owner * plen, plen), plen), pl.ds(chunk * width, width)]

    def token_copy(owner, chunk, to, send, recv):
        piece = tokens(owner, chunk)
        return pltpu.make_async_remote_copy(src_ref=piece, dst_ref=piece, send_sem=send.at[chunk], recv_sem=recv.at[chunk],
                                            device_id=(f, to), device_id_type=MESH)

    def pass_on(chunk):
        token_copy(across, chunk, across, n_send, n_recv).wait_recv()
        token_copy(across, chunk, brother, r_send, r_recv).start()

    send_gram(0, gram_u)
    load_w.wait()
    sends(1)
    pair(a).start()
    load_x.wait()
    for chunk in range(CHUNKS):
        token_copy(s, chunk, across, n_send, n_recv).start()
    for chunk in range(CHUNKS):
        token_copy(s, chunk, brother, b_send, b_recv).start()

    inv_u, inv_v = inverse_factors([sum_gram(0), gram_v])
    qu_ref[...] = exact(u_ref[...], inv_u, ((1,), (1,)))
    send_gram(1, exact(qu_ref[...], qu_ref[...], ((0,), (0,))))
    qv_ref[...] = exact(v_ref[...], inv_v, ((1,), (1,)))
    gram_v = exact(qv_ref[...], qv_ref[...], ((0,), (0,)))
    relay(1)
    pass_on(0)
    inv_u, inv_v = inverse_factors([sum_gram(1), gram_v])
    q_u = exact(qu_ref[...], inv_u, ((1,), (1,)))
    qu_ref[...] = q_u
    q_low = q_u.astype(BF)
    mine = qp.at[pl.ds(pl.multiple_of(f * half, half), half), :]
    mine[...] = jnp.concatenate([q_low[:half], q_low[half:]], axis=1)

    def low_copy(owner, d):
        piece = qp.at[pl.ds(pl.multiple_of(owner * half, half), half), :]
        return pltpu.make_async_remote_copy(src_ref=piece, dst_ref=piece, send_sem=q_send.at[d], recv_sem=q_recv.at[d],
                                            device_id=(lax.rem(f + d, nf), s), device_id_type=MESH)

    @pl.loop(1, nf)
    def _(d):
        low_copy(f, d).start()

    qv_ref[...] = exact(qv_ref[...], inv_v, ((1,), (1,)))
    pass_on(1)

    @pl.loop(2, line)
    def _(k):
        relay(k)

    for chunk in range(2, CHUNKS):
        pass_on(chunk)

    @pl.loop(1, nf)
    def _(d):
        low_copy(lax.rem(f + nf - d, nf), d).wait_recv()

    for i in range(nf):
        ql[i * rows : i * rows + half, :] = qp[i * half : (i + 1) * half, :R]
        ql[i * rows + half : (i + 1) * rows, :] = qp[i * half : (i + 1) * half, R:]

    for chunk in range(CHUNKS):
        token_copy(brother, chunk, brother, b_send, b_recv).wait_recv()
    far = lax.rem(brother + 2, ns)
    for chunk in range(CHUNKS):
        token_copy(far, chunk, brother, r_send, r_recv).wait_recv()

    @pl.loop(0, line)
    def _(at):
        pair_arrival(at).wait_recv()

    acc[...] = jnp.zeros_like(acc)
    sacc[...] = jnp.zeros_like(sacc)

    @pl.loop(0, D // KT)
    def _(t):
        at = pl.ds(pl.multiple_of(t * KT, KT), KT)
        piece = xs[:, at]
        acc[...] += dot(piece, ws[at, :], ((1,), (0,)))
        sacc[...] += dot(piece, ql[at, :], ((1,), (0,)))

    v_slice = qv_ref[pl.ds(pl.multiple_of(s * cols, cols), cols), :]
    offset = 2.0 * exact(sacc[...], v_slice, ((1,), (1,)))
    keys_ref[0] = (acc[...] + offset).astype(BF)
    keys_ref[1] = (acc[...] - offset).astype(BF)

    for turn in range(2):
        @pl.loop(1, nf)
        def _(d):
            gram_copy(turn, d).wait_send()

    @pl.loop(1, nf)
    def _(d):
        low_copy(f, d).wait_send()

    @pl.loop(1, line)
    def _(k):
        @pl.when((a + 1 < line) & (a - k + 1 >= 0))
        def _():
            up(k).wait_send()

        @pl.when((a > 0) & (a + k - 1 < line))
        def _():
            down(k).wait_send()

    @pl.loop(0, line)
    def _(at):
        pair(at).wait_send()

    for chunk in range(CHUNKS):
        token_copy(s, chunk, across, n_send, n_recv).wait_send()
        token_copy(s, chunk, brother, b_send, b_recv).wait_send()
        token_copy(across, chunk, brother, r_send, r_recv).wait_send()


def compute_keys(nf, ns, tokens, key_weight, u_factor, v_factor):
    length = tokens.shape[1] * ns
    rows, cols = key_weight.shape
    dma = lambda *n: pltpu.SemaphoreType.DMA(n)
    line = nf // 2
    return pl.pallas_call(
        functools.partial(keys_kernel, nf, ns),
        out_shape=(
            jax.ShapeDtypeStruct((2, length, cols), BF),
            jax.ShapeDtypeStruct((rows, R), F32),
            jax.ShapeDtypeStruct((KD, R), F32),
        ),
        in_specs=[ANY, ANY, VMEM, VMEM],
        out_specs=(VMEM, VMEM, VMEM),
        scratch_shapes=[
            pltpu.VMEM((length, D), BF),
            pltpu.VMEM((D, cols), BF),
            pltpu.VMEM((D // 2, 2 * R), BF),
            pltpu.VMEM((D, R), BF),
            pltpu.VMEM((2, nf, R, R), F32),
            pltpu.VMEM((length, cols), F32),
            pltpu.VMEM((length, R), F32),
            dma(2), dma(2, nf), dma(2, nf), dma(nf), dma(nf),
            dma(line + 1), dma(line + 1), dma(line + 1), dma(line + 1), dma(line), dma(line),
            dma(CHUNKS), dma(CHUNKS), dma(CHUNKS), dma(CHUNKS), dma(CHUNKS), dma(CHUNKS),
        ],
        compiler_params=pltpu.CompilerParams(collective_id=0, has_side_effects=True, vmem_limit_bytes=48 << 20),
        cost_estimate=pl.CostEstimate(flops=2 * length * D * (cols + R), bytes_accessed=16 << 20, transcendentals=0),
    )(tokens, key_weight, u_factor, v_factor)


def attention_kernel(heads, q_ref, k_ref, u_ref, v_ref, sums_ref, update_ref):
    step = pl.program_id(0)
    length = q_ref.shape[0]
    tile = 256
    scale = 1.0 / math.sqrt(HD)
    twice = scale * math.log2(math.e)

    @pl.when(step == 0)
    def _():
        sums_ref[...] = jnp.zeros_like(sums_ref)

    def parts(value):
        high = value.astype(BF)
        return high, (value - high.astype(F32)).astype(BF)

    u_high, u_rest = parts(u_ref[...])
    v_high, v_rest = parts(v_ref[...])
    product = dot(jnp.concatenate([u_high, u_rest, u_high], axis=1), jnp.concatenate([v_high, v_high, v_rest], axis=1), ((1,), (1,)))
    update_ref[...] = math.sqrt(D * KD / R) * product

    keep = lax.broadcasted_iota(jnp.int32, (tile, tile), 0) <= lax.broadcasted_iota(jnp.int32, (tile, tile), 1)
    for head in range(heads):
        for start in range(0, length, tile):
            q = q_ref[start : start + tile, head * HD : (head + 1) * HD]
            for p in range(2):
                last = dot(k_ref[p, start : start + tile, :], q, ((1,), (1,)))
                last = jnp.where(keep, last, -1e30)
                top = jnp.max(last, axis=0, keepdims=True)
                if start > 0:
                    before = dot(k_ref[p, :start, :], q, ((1,), (1,)))
                    top = jnp.maximum(top, jnp.max(before, axis=0, keepdims=True))
                total = jnp.sum(jnp.exp2((last - top) * twice), axis=0, keepdims=True)
                if start > 0:
                    total += jnp.sum(jnp.exp2((before - top) * twice), axis=0, keepdims=True)
                sums_ref[p : p + 1, start : start + tile] += top * scale + jnp.log(total)


def attend(query_rows, keys, q_u, q_v):
    length, width = query_rows.shape
    rows = q_u.shape[0]
    steps = 8
    heads = width // HD // steps
    return pl.pallas_call(
        functools.partial(attention_kernel, heads),
        grid=(steps,),
        out_shape=(jax.ShapeDtypeStruct((8, length), F32), jax.ShapeDtypeStruct((rows, KD), F32)),
        in_specs=[
            pl.BlockSpec((length, heads * HD), lambda i: (0, i)),
            pl.BlockSpec((2, length, HD), lambda i: (0, 0, i * heads // GROUP)),
            pl.BlockSpec((rows // steps, R), lambda i: (i, 0)),
            pl.BlockSpec((KD, R), lambda i: (0, 0)),
        ],
        out_specs=(pl.BlockSpec((8, length), lambda i: (0, 0)), pl.BlockSpec((rows // steps, KD), lambda i: (i, 0))),
        compiler_params=pltpu.CompilerParams(dimension_semantics=("arbitrary",), vmem_limit_bytes=32 << 20),
    )(query_rows, keys, q_u, q_v)


def loss_kernel(nf, ns, divisor, sums_ref, out_ref, over_f, over_s, f_send, f_recv, s_send, s_recv):
    f = lax.axis_index("fsdp")
    s = lax.axis_index("seq")
    barrier = pltpu.get_barrier_semaphore()

    @pl.loop(1, nf)
    def _(d):
        pl.semaphore_signal(barrier, inc=1, device_id=(lax.rem(f + d, nf), s), device_id_type=MESH)

    @pl.loop(1, ns)
    def _(d):
        pl.semaphore_signal(barrier, inc=1, device_id=(f, lax.rem(s + d, ns)), device_id_type=MESH)

    length = sums_ref.shape[1]
    over_s[s] = sum(sums_ref[:, at : at + 128] for at in range(0, length, 128))
    pl.semaphore_wait(barrier, nf - 1 + ns - 1)

    def copy_s(owner, d):
        return pltpu.make_async_remote_copy(src_ref=over_s.at[owner], dst_ref=over_s.at[owner], send_sem=s_send.at[d],
                                            recv_sem=s_recv.at[d], device_id=(f, lax.rem(s + d, ns)), device_id_type=MESH)

    def copy_f(owner, d):
        return pltpu.make_async_remote_copy(src_ref=over_f.at[owner], dst_ref=over_f.at[owner], send_sem=f_send.at[d],
                                            recv_sem=f_recv.at[d], device_id=(lax.rem(f + d, nf), s), device_id_type=MESH)

    @pl.loop(1, ns)
    def _(d):
        copy_s(s, d).start()

    @pl.loop(1, ns)
    def _(d):
        copy_s(lax.rem(s + ns - d, ns), d).wait_recv()

    over_f[f] = jnp.sum(over_s[...], axis=0)

    @pl.loop(1, nf)
    def _(d):
        copy_f(f, d).start()

    @pl.loop(1, nf)
    def _(d):
        copy_f(lax.rem(f + nf - d, nf), d).wait_recv()

    whole = jnp.sum(over_f[...], axis=0)
    out_ref[...] = jnp.broadcast_to(jnp.sum(whole, axis=1, keepdims=True) * (1.0 / divisor), out_ref.shape)

    @pl.loop(1, ns)
    def _(d):
        copy_s(s, d).wait_send()

    @pl.loop(1, nf)
    def _(d):
        copy_f(f, d).wait_send()


def total_loss(nf, ns, sums, divisor):
    dma = lambda n: pltpu.SemaphoreType.DMA((n,))
    return pl.pallas_call(
        functools.partial(loss_kernel, nf, ns, divisor),
        out_shape=jax.ShapeDtypeStruct((8, 128), F32),
        in_specs=[VMEM],
        out_specs=VMEM,
        scratch_shapes=[pltpu.VMEM((nf, 8, 128), F32), pltpu.VMEM((ns, 8, 128), F32), dma(nf), dma(nf), dma(ns), dma(ns)],
        compiler_params=pltpu.CompilerParams(collective_id=1, has_side_effects=True),
    )(sums)


def solution(mesh):
    nf, ns = mesh.shape["fsdp"], mesh.shape["seq"]

    def local(tokens, queries, key_weight, u_factor, v_factor):
        length = tokens.shape[1] * ns
        keys, q_u, q_v = compute_keys(nf, ns, tokens, key_weight, u_factor, v_factor)
        sums, update = attend(queries[0], keys, q_u, q_v)
        losses = total_loss(nf, ns, sums, float(nf * length * HQ))
        return update, losses[:2, 0]

    in_specs = (
        P("fsdp", "seq", None),
        P("fsdp", None, "seq"),
        P("fsdp", "seq"),
        P("fsdp", None),
        P(),
    )
    out_specs = (P("fsdp", None), P())
    return jax.shard_map(local, mesh=mesh, in_specs=in_specs, out_specs=out_specs, check_vma=False)
```

```python
import functools
import math

import jax
import jax.numpy as jnp
from jax import lax
from jax.experimental import pallas as pl
from jax.experimental.pallas import tpu as pltpu
from jax.sharding import PartitionSpec as P

D = 8192
HQ = 64
HD = 128
R = 64
KD = 1024
GROUP = 8
CHUNKS = 4
KT = 1024
BF = jnp.bfloat16
F32 = jnp.float32
MESH = pl.DeviceIdType.MESH
VMEM = pl.BlockSpec(memory_space=pltpu.VMEM)
ANY = pl.BlockSpec(memory_space=pl.ANY)


def dot(left, right, contract, precision=None):
    return lax.dot_general(left, right, ((contract[0], contract[1]), ((), ())), precision=precision, preferred_element_type=F32)


def exact(left, right, contract):
    return dot(left, right, contract, lax.Precision.HIGHEST)


def inverse_factors(grams):
    rows = lax.broadcasted_iota(jnp.int32, (R, 2 * R), 0)
    lanes = lax.broadcasted_iota(jnp.int32, (R, 2 * R), 1)
    unit = (lanes == rows + R).astype(F32)
    work = [jnp.concatenate([g, jnp.zeros((R, R), F32)], axis=1) + unit for g in grams]
    scales = [jnp.ones((R, 1), F32) for _ in grams]
    column_rows = lax.broadcasted_iota(jnp.int32, (R, 1), 0)
    for j in range(R):
        for n in range(len(work)):
            a = work[n]
            row = a[j : j + 1, :]
            column = a[:, j : j + 1]
            pivot = a[j : j + 1, j : j + 1]
            factor = jnp.where(column_rows > j, column * (1.0 / pivot), 0.0)
            scales[n] = jnp.where(column_rows == j, pivot, scales[n])
            work[n] = a - factor * row
    return [(a * lax.rsqrt(s))[:, R:] for a, s in zip(work, scales)]


def keys_kernel(nf, ns, x_hbm, w_hbm, u_ref, v_ref, keys_ref, qu_ref, qv_ref, xs, ws, qt, ql, ut, vt, gm, acc, sacc,
                in_sem, g_send, g_recv, q_send, q_recv, up_send, up_recv, dn_send, dn_recv, p_send, p_recv,
                b_send, b_recv, n_send, n_recv, r_send, r_recv, l_send, l_recv):
    f = lax.axis_index("fsdp")
    s = lax.axis_index("seq")
    line = nf // 2
    a, b = f // 2, lax.rem(f, 2)
    mate = 2 * a + (1 - b)
    core = lax.rem(s, 2)
    brother = s - core + (1 - core)
    across = lax.rem(s + 2, ns)
    rows = u_ref.shape[1]
    share, _, _, part = qt.shape
    own = s if share > 1 else 0
    plen = xs.shape[0] // ns
    width = D // CHUNKS
    cols = ws.shape[1]

    load_x = pltpu.make_async_copy(x_hbm.at[0], xs.at[pl.ds(pl.multiple_of(s * plen, plen), plen), :], in_sem.at[0])
    load_w = pltpu.make_async_copy(w_hbm, ws.at[pl.ds(pl.multiple_of(f * rows, rows), rows), :], in_sem.at[1])
    load_x.start()
    load_w.start()

    barrier = pltpu.get_barrier_semaphore()

    @pl.loop(1, nf)
    def _(d):
        pl.semaphore_signal(barrier, inc=1, device_id=(lax.rem(f + d, nf), s), device_id_type=MESH)

    @pl.loop(1, ns)
    def _(d):
        pl.semaphore_signal(barrier, inc=1, device_id=(f, lax.rem(s + d, ns)), device_id_type=MESH)

    pl.semaphore_wait(barrier, nf - 1 + ns - 1)

    def gram_copy(turn, d):
        return pltpu.make_async_remote_copy(
            src_ref=gm.at[turn, f], dst_ref=gm.at[turn, f], send_sem=g_send.at[turn, d], recv_sem=g_recv.at[turn, d],
            device_id=(lax.rem(f + d, nf), s), device_id_type=MESH)

    def gram_arrival(turn, d):
        source = lax.rem(f + nf - d, nf)
        return pltpu.make_async_remote_copy(
            src_ref=gm.at[turn, source], dst_ref=gm.at[turn, source], send_sem=g_send.at[turn, d],
            recv_sem=g_recv.at[turn, d], device_id=(lax.rem(f + d, nf), s), device_id_type=MESH)

    def send_gram(turn, gram):
        gm[turn, f] = gram

        @pl.loop(1, nf)
        def _(d):
            gram_copy(turn, d).start()

    def sum_gram(turn):
        @pl.loop(1, nf)
        def _(d):
            gram_arrival(turn, d).wait_recv()

        return jnp.sum(gm[turn], axis=0)

    def block(index):
        return ws.at[pl.ds(pl.multiple_of(index * rows, rows), rows), :]

    def up(k):
        piece = block(2 * (a - k + 1) + b)
        return pltpu.make_async_remote_copy(src_ref=piece, dst_ref=piece, send_sem=up_send.at[k], recv_sem=up_recv.at[k],
                                            device_id=(f + 2, s), device_id_type=MESH)

    def down(k):
        piece = block(2 * (a + k - 1) + b)
        return pltpu.make_async_remote_copy(src_ref=piece, dst_ref=piece, send_sem=dn_send.at[k], recv_sem=dn_recv.at[k],
                                            device_id=(f - 2, s), device_id_type=MESH)

    def pair(at):
        piece = block(2 * at + b)
        return pltpu.make_async_remote_copy(src_ref=piece, dst_ref=piece, send_sem=p_send.at[at], recv_sem=p_recv.at[at],
                                            device_id=(mate, s), device_id_type=MESH)

    def pair_arrival(at):
        piece = block(2 * at + (1 - b))
        return pltpu.make_async_remote_copy(src_ref=piece, dst_ref=piece, send_sem=p_send.at[at], recv_sem=p_recv.at[at],
                                            device_id=(mate, s), device_id_type=MESH)

    def sends(k):
        @pl.when((a + 1 < line) & (a - k + 1 >= 0))
        def _():
            up(k).start()

        @pl.when((a > 0) & (a + k - 1 < line))
        def _():
            down(k).start()

    def relay(k):
        @pl.when(a - k >= 0)
        def _():
            piece = block(2 * (a - k) + b)
            pltpu.make_async_remote_copy(src_ref=piece, dst_ref=piece, send_sem=up_send.at[k], recv_sem=up_recv.at[k],
                                         device_id=(mate, s), device_id_type=MESH).wait_recv()

        @pl.when(a + k < line)
        def _():
            piece = block(2 * (a + k) + b)
            pltpu.make_async_remote_copy(src_ref=piece, dst_ref=piece, send_sem=dn_send.at[k], recv_sem=dn_recv.at[k],
                                         device_id=(mate, s), device_id_type=MESH).wait_recv()

        sends(k + 1)

        @pl.when(a - k >= 0)
        def _():
            pair(a - k).start()

        @pl.when(a + k < line)
        def _():
            pair(a + k).start()

    def tokens(owner, chunk):
        return xs.at[pl.ds(pl.multiple_of(owner * plen, plen), plen), pl.ds(chunk * width, width)]

    def token_copy(owner, chunk, to, send, recv):
        piece = tokens(owner, chunk)
        return pltpu.make_async_remote_copy(src_ref=piece, dst_ref=piece, send_sem=send.at[chunk], recv_sem=recv.at[chunk],
                                            device_id=(f, to), device_id_type=MESH)

    def pass_on(chunk):
        token_copy(across, chunk, across, n_send, n_recv).wait_recv()
        token_copy(across, chunk, brother, r_send, r_recv).start()

    load_w.wait()
    sends(1)
    pair(a).start()
    load_x.wait()
    for chunk in range(CHUNKS):
        token_copy(s, chunk, across, n_send, n_recv).start()
    send_gram(0, exact(u_ref[...], u_ref[...], ((1,), (1,))))
    for chunk in range(CHUNKS):
        token_copy(s, chunk, brother, b_send, b_recv).start()

    gram_v = exact(v_ref[...], v_ref[...], ((1,), (1,)))
    inv_u, inv_v = inverse_factors([sum_gram(0), gram_v])
    ut[...] = exact(inv_u, u_ref[...], ((1,), (0,)))
    send_gram(1, exact(ut[...], ut[...], ((1,), (1,))))
    vt[...] = exact(inv_v, v_ref[...], ((1,), (0,)))
    gram_v = exact(vt[...], vt[...], ((1,), (1,)))
    relay(1)
    pass_on(0)
    inv_u, inv_v = inverse_factors([sum_gram(1), gram_v])
    ut[...] = exact(inv_u, ut[...], ((1,), (0,)))
    for j in range(share):
        @pl.when(own == j)
        def _():
            qt[j, f] = ut[:, j * part : (j + 1) * part].astype(BF)

    def low_copy(owner, d):
        piece = qt.at[own, owner]
        return pltpu.make_async_remote_copy(src_ref=piece, dst_ref=piece, send_sem=q_send.at[d], recv_sem=q_recv.at[d],
                                            device_id=(lax.rem(f + d, nf), s), device_id_type=MESH)

    def share_copy(owner, at, to):
        piece = qt.at[owner]
        return pltpu.make_async_remote_copy(src_ref=piece, dst_ref=piece, send_sem=l_send.at[at], recv_sem=l_recv.at[at],
                                            device_id=(f, to), device_id_type=MESH)

    @pl.loop(1, nf)
    def _(d):
        low_copy(f, d).start()

    vt[...] = exact(inv_v, vt[...], ((1,), (0,)))
    qu_ref[...] = ut[...].T
    qv_ref[...] = vt[...].T
    pass_on(1)
    if line > 2:
        relay(2)

    @pl.loop(1, nf)
    def _(d):
        low_copy(lax.rem(f + nf - d, nf), d).wait_recv()

    if share > 1:
        share_copy(own, 0, across).start()
        share_copy(own, 1, brother).start()

    @pl.loop(3, line)
    def _(k):
        relay(k)

    pass_on(2)
    if share > 1:
        share_copy(across, 0, across).wait_recv()
        share_copy(across, 2, brother).start()
    pass_on(3)

    far = lax.rem(brother + 2, ns)
    if share > 1:
        share_copy(brother, 1, brother).wait_recv()
        share_copy(far, 2, brother).wait_recv()
    for i in range(nf):
        for j in range(share):
            at = i * rows + j * part
            ql[:, at : at + part] = qt[j, i]

    for chunk in range(CHUNKS):
        token_copy(brother, chunk, brother, b_send, b_recv).wait_recv()
    for chunk in range(CHUNKS):
        token_copy(far, chunk, brother, r_send, r_recv).wait_recv()

    @pl.loop(0, line)
    def _(at):
        pair_arrival(at).wait_recv()

    acc[...] = jnp.zeros_like(acc)
    sacc[...] = jnp.zeros_like(sacc)

    @pl.loop(0, D // KT)
    def _(t):
        at = pl.ds(pl.multiple_of(t * KT, KT), KT)
        piece = xs[:, at]
        acc[...] += dot(piece, ws[at, :], ((1,), (0,)))
        sacc[...] += dot(piece, ql[:, at], ((1,), (1,)))

    v_slice = vt[:, pl.ds(pl.multiple_of(s * cols, cols), cols)]
    offset = 2.0 * exact(sacc[...], v_slice, ((1,), (0,)))
    keys_ref[0] = (acc[...] + offset).astype(BF)
    keys_ref[1] = (acc[...] - offset).astype(BF)

    for turn in range(2):
        @pl.loop(1, nf)
        def _(d):
            gram_copy(turn, d).wait_send()

    @pl.loop(1, nf)
    def _(d):
        low_copy(f, d).wait_send()

    @pl.loop(1, line)
    def _(k):
        @pl.when((a + 1 < line) & (a - k + 1 >= 0))
        def _():
            up(k).wait_send()

        @pl.when((a > 0) & (a + k - 1 < line))
        def _():
            down(k).wait_send()

    @pl.loop(0, line)
    def _(at):
        pair(at).wait_send()

    for chunk in range(CHUNKS):
        token_copy(s, chunk, across, n_send, n_recv).wait_send()
        token_copy(s, chunk, brother, b_send, b_recv).wait_send()
        token_copy(across, chunk, brother, r_send, r_recv).wait_send()
    if share > 1:
        share_copy(own, 0, across).wait_send()
        share_copy(own, 1, brother).wait_send()
        share_copy(across, 2, brother).wait_send()


def compute_keys(nf, ns, tokens, key_weight, u_factor, v_factor):
    length = tokens.shape[1] * ns
    rows, cols = key_weight.shape
    dma = lambda *n: pltpu.SemaphoreType.DMA(n)
    line = nf // 2
    share = ns if rows % (128 * ns) == 0 else 1
    return pl.pallas_call(
        functools.partial(keys_kernel, nf, ns),
        out_shape=(
            jax.ShapeDtypeStruct((2, length, cols), BF),
            jax.ShapeDtypeStruct((rows, R), F32),
            jax.ShapeDtypeStruct((KD, R), F32),
        ),
        in_specs=[ANY, ANY, VMEM, VMEM],
        out_specs=(VMEM, VMEM, VMEM),
        scratch_shapes=[
            pltpu.VMEM((length, D), BF),
            pltpu.VMEM((D, cols), BF),
            pltpu.VMEM((share, nf, R, rows // share), BF),
            pltpu.VMEM((R, D), BF),
            pltpu.VMEM((R, rows), F32),
            pltpu.VMEM((R, KD), F32),
            pltpu.VMEM((2, nf, R, R), F32),
            pltpu.VMEM((length, cols), F32),
            pltpu.VMEM((length, R), F32),
            dma(2), dma(2, nf), dma(2, nf), dma(nf), dma(nf),
            dma(line + 1), dma(line + 1), dma(line + 1), dma(line + 1), dma(line), dma(line),
            dma(CHUNKS), dma(CHUNKS), dma(CHUNKS), dma(CHUNKS), dma(CHUNKS), dma(CHUNKS), dma(3), dma(3),
        ],
        compiler_params=pltpu.CompilerParams(collective_id=0, has_side_effects=True, vmem_limit_bytes=60 << 20),
        cost_estimate=pl.CostEstimate(flops=2 * length * D * (cols + R), bytes_accessed=16 << 20, transcendentals=0),
    )(tokens, key_weight, u_factor.T, v_factor.T)


def attention_kernel(heads, q_ref, k_ref, u_ref, v_ref, sums_ref, update_ref):
    step = pl.program_id(0)
    length = q_ref.shape[0]
    tile = 256
    scale = 1.0 / math.sqrt(HD)
    twice = scale * math.log2(math.e)

    @pl.when(step == 0)
    def _():
        sums_ref[...] = jnp.zeros_like(sums_ref)

    def parts(value):
        high = value.astype(BF)
        return high, (value - high.astype(F32)).astype(BF)

    u_high, u_rest = parts(u_ref[...])
    v_high, v_rest = parts(v_ref[...])
    product = dot(jnp.concatenate([u_high, u_rest, u_high], axis=1), jnp.concatenate([v_high, v_high, v_rest], axis=1), ((1,), (1,)))
    update_ref[...] = math.sqrt(D * KD / R) * product

    keep = lax.broadcasted_iota(jnp.int32, (tile, tile), 0) <= lax.broadcasted_iota(jnp.int32, (tile, tile), 1)
    for head in range(heads):
        for start in range(0, length, tile):
            q = q_ref[start : start + tile, head * HD : (head + 1) * HD]
            for p in range(2):
                last = dot(k_ref[p, start : start + tile, :], q, ((1,), (1,)))
                last = jnp.where(keep, last, -1e30)
                top = jnp.max(last, axis=0, keepdims=True)
                if start > 0:
                    before = dot(k_ref[p, :start, :], q, ((1,), (1,)))
                    top = jnp.maximum(top, jnp.max(before, axis=0, keepdims=True))
                total = jnp.sum(jnp.exp2((last - top) * twice), axis=0, keepdims=True)
                if start > 0:
                    total += jnp.sum(jnp.exp2((before - top) * twice), axis=0, keepdims=True)
                sums_ref[p : p + 1, start : start + tile] += top * scale + jnp.log(total)


def attend(query_rows, keys, q_u, q_v):
    length, width = query_rows.shape
    rows = q_u.shape[0]
    steps = 8
    heads = width // HD // steps
    return pl.pallas_call(
        functools.partial(attention_kernel, heads),
        grid=(steps,),
        out_shape=(jax.ShapeDtypeStruct((8, length), F32), jax.ShapeDtypeStruct((rows, KD), F32)),
        in_specs=[
            pl.BlockSpec((length, heads * HD), lambda i: (0, i)),
            pl.BlockSpec((2, length, HD), lambda i: (0, 0, i * heads // GROUP)),
            pl.BlockSpec((rows // steps, R), lambda i: (i, 0)),
            pl.BlockSpec((KD, R), lambda i: (0, 0)),
        ],
        out_specs=(pl.BlockSpec((8, length), lambda i: (0, 0)), pl.BlockSpec((rows // steps, KD), lambda i: (i, 0))),
        compiler_params=pltpu.CompilerParams(dimension_semantics=("arbitrary",), vmem_limit_bytes=32 << 20),
    )(query_rows, keys, q_u, q_v)


def loss_kernel(nf, ns, divisor, sums_ref, out_ref, over_f, over_s, f_send, f_recv, s_send, s_recv):
    f = lax.axis_index("fsdp")
    s = lax.axis_index("seq")
    barrier = pltpu.get_barrier_semaphore()

    @pl.loop(1, nf)
    def _(d):
        pl.semaphore_signal(barrier, inc=1, device_id=(lax.rem(f + d, nf), s), device_id_type=MESH)

    @pl.loop(1, ns)
    def _(d):
        pl.semaphore_signal(barrier, inc=1, device_id=(f, lax.rem(s + d, ns)), device_id_type=MESH)

    length = sums_ref.shape[1]
    over_s[s] = sum(sums_ref[:, at : at + 128] for at in range(0, length, 128))
    pl.semaphore_wait(barrier, nf - 1 + ns - 1)

    def copy_s(owner, d):
        return pltpu.make_async_remote_copy(src_ref=over_s.at[owner], dst_ref=over_s.at[owner], send_sem=s_send.at[d],
                                            recv_sem=s_recv.at[d], device_id=(f, lax.rem(s + d, ns)), device_id_type=MESH)

    def copy_f(owner, d):
        return pltpu.make_async_remote_copy(src_ref=over_f.at[owner], dst_ref=over_f.at[owner], send_sem=f_send.at[d],
                                            recv_sem=f_recv.at[d], device_id=(lax.rem(f + d, nf), s), device_id_type=MESH)

    @pl.loop(1, ns)
    def _(d):
        copy_s(s, d).start()

    @pl.loop(1, ns)
    def _(d):
        copy_s(lax.rem(s + ns - d, ns), d).wait_recv()

    over_f[f] = jnp.sum(over_s[...], axis=0)

    @pl.loop(1, nf)
    def _(d):
        copy_f(f, d).start()

    @pl.loop(1, nf)
    def _(d):
        copy_f(lax.rem(f + nf - d, nf), d).wait_recv()

    whole = jnp.sum(over_f[...], axis=0)
    out_ref[...] = jnp.broadcast_to(jnp.sum(whole, axis=1, keepdims=True) * (1.0 / divisor), out_ref.shape)

    @pl.loop(1, ns)
    def _(d):
        copy_s(s, d).wait_send()

    @pl.loop(1, nf)
    def _(d):
        copy_f(f, d).wait_send()


def total_loss(nf, ns, sums, divisor):
    dma = lambda n: pltpu.SemaphoreType.DMA((n,))
    return pl.pallas_call(
        functools.partial(loss_kernel, nf, ns, divisor),
        out_shape=jax.ShapeDtypeStruct((8, 128), F32),
        in_specs=[VMEM],
        out_specs=VMEM,
        scratch_shapes=[pltpu.VMEM((nf, 8, 128), F32), pltpu.VMEM((ns, 8, 128), F32), dma(nf), dma(nf), dma(ns), dma(ns)],
        compiler_params=pltpu.CompilerParams(collective_id=1, has_side_effects=True),
    )(sums)


def solution(mesh):
    nf, ns = mesh.shape["fsdp"], mesh.shape["seq"]

    def local(tokens, queries, key_weight, u_factor, v_factor):
        length = tokens.shape[1] * ns
        keys, q_u, q_v = compute_keys(nf, ns, tokens, key_weight, u_factor, v_factor)
        sums, update = attend(queries[0], keys, q_u, q_v)
        losses = total_loss(nf, ns, sums, float(nf * length * HQ))
        return update, losses[:2, 0]

    in_specs = (
        P("fsdp", "seq", None),
        P("fsdp", None, "seq"),
        P("fsdp", "seq"),
        P("fsdp", None),
        P(),
    )
    out_specs = (P("fsdp", None), P())
    return jax.shard_map(local, mesh=mesh, in_specs=in_specs, out_specs=out_specs, check_vma=False)
```

```python
import functools
import math

import jax
import jax.numpy as jnp
from jax import lax
from jax.experimental import pallas as pl
from jax.experimental.pallas import tpu as pltpu
from jax.sharding import PartitionSpec as P

D = 8192
HQ = 64
HD = 128
R = 64
KD = 1024
GROUP = 8
CHUNKS = 4
KT = 1024
BF = jnp.bfloat16
F32 = jnp.float32
MESH = pl.DeviceIdType.MESH
VMEM = pl.BlockSpec(memory_space=pltpu.VMEM)
ANY = pl.BlockSpec(memory_space=pl.ANY)


def dot(left, right, contract, precision=None):
    return lax.dot_general(left, right, ((contract[0], contract[1]), ((), ())), precision=precision, preferred_element_type=F32)


def exact(left, right, contract):
    return dot(left, right, contract, lax.Precision.HIGHEST)


def inverse_factors(grams):
    rows = lax.broadcasted_iota(jnp.int32, (R, 2 * R), 0)
    lanes = lax.broadcasted_iota(jnp.int32, (R, 2 * R), 1)
    unit = (lanes == rows + R).astype(F32)
    work = [jnp.concatenate([g, jnp.zeros((R, R), F32)], axis=1) + unit for g in grams]
    scales = [jnp.ones((R, 1), F32) for _ in grams]
    column_rows = lax.broadcasted_iota(jnp.int32, (R, 1), 0)
    for j in range(R):
        for n in range(len(work)):
            a = work[n]
            row = a[j : j + 1, :]
            column = a[:, j : j + 1]
            pivot = a[j : j + 1, j : j + 1]
            factor = jnp.where(column_rows > j, column * (1.0 / pivot), 0.0)
            scales[n] = jnp.where(column_rows == j, pivot, scales[n])
            work[n] = a - factor * row
    return [(a * lax.rsqrt(s))[:, R:] for a, s in zip(work, scales)]


def keys_kernel(nf, ns, x_hbm, w_hbm, u_ref, v_ref, keys_ref, qu_ref, qv_ref, xs, ws, qt, ql, ut, vt, gm, acc, sacc,
                in_sem, g_send, g_recv, q_send, q_recv, up_send, up_recv, dn_send, dn_recv, p_send, p_recv,
                b_send, b_recv, n_send, n_recv, r_send, r_recv, l_send, l_recv):
    f = lax.axis_index("fsdp")
    s = lax.axis_index("seq")
    line = nf // 2
    a, b = f // 2, lax.rem(f, 2)
    mate = 2 * a + (1 - b)
    core = lax.rem(s, 2)
    brother = s - core + (1 - core)
    across = lax.rem(s + 2, ns)
    rows = u_ref.shape[1]
    share, _, _, part = qt.shape
    own = s if share > 1 else 0
    plen = xs.shape[0] // ns
    width = D // CHUNKS
    cols = ws.shape[1]

    load_x = pltpu.make_async_copy(x_hbm.at[0], xs.at[pl.ds(pl.multiple_of(s * plen, plen), plen), :], in_sem.at[0])
    load_w = pltpu.make_async_copy(w_hbm, ws.at[pl.ds(pl.multiple_of(f * rows, rows), rows), :], in_sem.at[1])
    load_x.start()
    load_w.start()

    barrier = pltpu.get_barrier_semaphore()

    @pl.loop(1, nf)
    def _(d):
        pl.semaphore_signal(barrier, inc=1, device_id=(lax.rem(f + d, nf), s), device_id_type=MESH)

    @pl.loop(1, ns)
    def _(d):
        pl.semaphore_signal(barrier, inc=1, device_id=(f, lax.rem(s + d, ns)), device_id_type=MESH)

    pl.semaphore_wait(barrier, nf - 1 + ns - 1)

    def gram_copy(turn, d):
        return pltpu.make_async_remote_copy(
            src_ref=gm.at[turn, f], dst_ref=gm.at[turn, f], send_sem=g_send.at[turn, d], recv_sem=g_recv.at[turn, d],
            device_id=(lax.rem(f + d, nf), s), device_id_type=MESH)

    def gram_arrival(turn, d):
        source = lax.rem(f + nf - d, nf)
        return pltpu.make_async_remote_copy(
            src_ref=gm.at[turn, source], dst_ref=gm.at[turn, source], send_sem=g_send.at[turn, d],
            recv_sem=g_recv.at[turn, d], device_id=(lax.rem(f + d, nf), s), device_id_type=MESH)

    def send_gram(turn, gram):
        gm[turn, f] = gram

        @pl.loop(1, nf)
        def _(d):
            gram_copy(turn, d).start()

    def sum_gram(turn):
        @pl.loop(1, nf)
        def _(d):
            gram_arrival(turn, d).wait_recv()

        return jnp.sum(gm[turn], axis=0)

    def block(index):
        return ws.at[pl.ds(pl.multiple_of(index * rows, rows), rows), :]

    def up(k):
        piece = block(2 * (a - k + 1) + b)
        return pltpu.make_async_remote_copy(src_ref=piece, dst_ref=piece, send_sem=up_send.at[k], recv_sem=up_recv.at[k],
                                            device_id=(f + 2, s), device_id_type=MESH)

    def down(k):
        piece = block(2 * (a + k - 1) + b)
        return pltpu.make_async_remote_copy(src_ref=piece, dst_ref=piece, send_sem=dn_send.at[k], recv_sem=dn_recv.at[k],
                                            device_id=(f - 2, s), device_id_type=MESH)

    def pair(at):
        piece = block(2 * at + b)
        return pltpu.make_async_remote_copy(src_ref=piece, dst_ref=piece, send_sem=p_send.at[at], recv_sem=p_recv.at[at],
                                            device_id=(mate, s), device_id_type=MESH)

    def pair_arrival(at):
        piece = block(2 * at + (1 - b))
        return pltpu.make_async_remote_copy(src_ref=piece, dst_ref=piece, send_sem=p_send.at[at], recv_sem=p_recv.at[at],
                                            device_id=(mate, s), device_id_type=MESH)

    def sends(k):
        @pl.when((a + 1 < line) & (a - k + 1 >= 0))
        def _():
            up(k).start()

        @pl.when((a > 0) & (a + k - 1 < line))
        def _():
            down(k).start()

    def relay(k):
        @pl.when(a - k >= 0)
        def _():
            piece = block(2 * (a - k) + b)
            pltpu.make_async_remote_copy(src_ref=piece, dst_ref=piece, send_sem=up_send.at[k], recv_sem=up_recv.at[k],
                                         device_id=(mate, s), device_id_type=MESH).wait_recv()

        @pl.when(a + k < line)
        def _():
            piece = block(2 * (a + k) + b)
            pltpu.make_async_remote_copy(src_ref=piece, dst_ref=piece, send_sem=dn_send.at[k], recv_sem=dn_recv.at[k],
                                         device_id=(mate, s), device_id_type=MESH).wait_recv()

        sends(k + 1)

        @pl.when(a - k >= 0)
        def _():
            pair(a - k).start()

        @pl.when(a + k < line)
        def _():
            pair(a + k).start()

    def tokens(owner, chunk):
        return xs.at[pl.ds(pl.multiple_of(owner * plen, plen), plen), pl.ds(chunk * width, width)]

    def token_copy(owner, chunk, to, send, recv):
        piece = tokens(owner, chunk)
        return pltpu.make_async_remote_copy(src_ref=piece, dst_ref=piece, send_sem=send.at[chunk], recv_sem=recv.at[chunk],
                                            device_id=(f, to), device_id_type=MESH)

    def pass_on(chunk):
        token_copy(across, chunk, across, n_send, n_recv).wait_recv()
        token_copy(across, chunk, brother, r_send, r_recv).start()

    load_w.wait()
    sends(1)
    pair(a).start()
    load_x.wait()
    for chunk in range(CHUNKS):
        token_copy(s, chunk, across, n_send, n_recv).start()
    send_gram(0, exact(u_ref[...], u_ref[...], ((1,), (1,))))
    for chunk in range(CHUNKS):
        token_copy(s, chunk, brother, b_send, b_recv).start()

    gram_v = exact(v_ref[...], v_ref[...], ((1,), (1,)))
    inv_u, inv_v = inverse_factors([sum_gram(0), gram_v])
    ut[...] = exact(inv_u, u_ref[...], ((1,), (0,)))
    send_gram(1, exact(ut[...], ut[...], ((1,), (1,))))
    vt[...] = exact(inv_v, v_ref[...], ((1,), (0,)))
    gram_v = exact(vt[...], vt[...], ((1,), (1,)))
    relay(1)
    inv_u, inv_v = inverse_factors([sum_gram(1), gram_v])
    ut[...] = exact(inv_u, ut[...], ((1,), (0,)))
    for j in range(share):
        @pl.when(own == j)
        def _():
            qt[j, f] = ut[:, j * part : (j + 1) * part].astype(BF)

    def low_copy(owner, d):
        piece = qt.at[own, owner]
        return pltpu.make_async_remote_copy(src_ref=piece, dst_ref=piece, send_sem=q_send.at[d], recv_sem=q_recv.at[d],
                                            device_id=(lax.rem(f + d, nf), s), device_id_type=MESH)

    def share_copy(owner, at, to):
        piece = qt.at[owner]
        return pltpu.make_async_remote_copy(src_ref=piece, dst_ref=piece, send_sem=l_send.at[at], recv_sem=l_recv.at[at],
                                            device_id=(f, to), device_id_type=MESH)

    @pl.loop(1, nf)
    def _(d):
        low_copy(f, d).start()

    vt[...] = exact(inv_v, vt[...], ((1,), (0,)))
    qu_ref[...] = ut[...].T
    qv_ref[...] = vt[...].T
    if line > 2:
        relay(2)
    pass_on(0)
    pass_on(1)

    @pl.loop(1, nf)
    def _(d):
        low_copy(lax.rem(f + nf - d, nf), d).wait_recv()

    if share > 1:
        share_copy(own, 0, across).start()
        share_copy(own, 1, brother).start()

    @pl.loop(3, line)
    def _(k):
        relay(k)

    pass_on(2)
    if share > 1:
        share_copy(across, 0, across).wait_recv()
        share_copy(across, 2, brother).start()
    pass_on(3)

    far = lax.rem(brother + 2, ns)
    if share > 1:
        share_copy(brother, 1, brother).wait_recv()
        share_copy(far, 2, brother).wait_recv()
    for i in range(nf):
        for j in range(share):
            at = i * rows + j * part
            ql[:, at : at + part] = qt[j, i]

    for chunk in range(CHUNKS):
        token_copy(brother, chunk, brother, b_send, b_recv).wait_recv()
    for chunk in range(CHUNKS):
        token_copy(far, chunk, brother, r_send, r_recv).wait_recv()

    @pl.loop(0, line)
    def _(at):
        pair_arrival(at).wait_recv()

    acc[...] = jnp.zeros_like(acc)
    sacc[...] = jnp.zeros_like(sacc)

    @pl.loop(0, D // KT)
    def _(t):
        at = pl.ds(pl.multiple_of(t * KT, KT), KT)
        piece = xs[:, at]
        acc[...] += dot(piece, ws[at, :], ((1,), (0,)))
        sacc[...] += dot(piece, ql[:, at], ((1,), (1,)))

    v_slice = vt[:, pl.ds(pl.multiple_of(s * cols, cols), cols)]
    offset = 2.0 * exact(sacc[...], v_slice, ((1,), (0,)))
    keys_ref[0] = (acc[...] + offset).astype(BF)
    keys_ref[1] = (acc[...] - offset).astype(BF)

    for turn in range(2):
        @pl.loop(1, nf)
        def _(d):
            gram_copy(turn, d).wait_send()

    @pl.loop(1, nf)
    def _(d):
        low_copy(f, d).wait_send()

    @pl.loop(1, line)
    def _(k):
        @pl.when((a + 1 < line) & (a - k + 1 >= 0))
        def _():
            up(k).wait_send()

        @pl.when((a > 0) & (a + k - 1 < line))
        def _():
            down(k).wait_send()

    @pl.loop(0, line)
    def _(at):
        pair(at).wait_send()

    for chunk in range(CHUNKS):
        token_copy(s, chunk, across, n_send, n_recv).wait_send()
        token_copy(s, chunk, brother, b_send, b_recv).wait_send()
        token_copy(across, chunk, brother, r_send, r_recv).wait_send()
    if share > 1:
        share_copy(own, 0, across).wait_send()
        share_copy(own, 1, brother).wait_send()
        share_copy(across, 2, brother).wait_send()


def compute_keys(nf, ns, tokens, key_weight, u_factor, v_factor):
    length = tokens.shape[1] * ns
    rows, cols = key_weight.shape
    dma = lambda *n: pltpu.SemaphoreType.DMA(n)
    line = nf // 2
    share = ns if rows % (128 * ns) == 0 else 1
    return pl.pallas_call(
        functools.partial(keys_kernel, nf, ns),
        out_shape=(
            jax.ShapeDtypeStruct((2, length, cols), BF),
            jax.ShapeDtypeStruct((rows, R), F32),
            jax.ShapeDtypeStruct((KD, R), F32),
        ),
        in_specs=[ANY, ANY, VMEM, VMEM],
        out_specs=(VMEM, VMEM, VMEM),
        scratch_shapes=[
            pltpu.VMEM((length, D), BF),
            pltpu.VMEM((D, cols), BF),
            pltpu.VMEM((share, nf, R, rows // share), BF),
            pltpu.VMEM((R, D), BF),
            pltpu.VMEM((R, rows), F32),
            pltpu.VMEM((R, KD), F32),
            pltpu.VMEM((2, nf, R, R), F32),
            pltpu.VMEM((length, cols), F32),
            pltpu.VMEM((length, R), F32),
            dma(2), dma(2, nf), dma(2, nf), dma(nf), dma(nf),
            dma(line + 1), dma(line + 1), dma(line + 1), dma(line + 1), dma(line), dma(line),
            dma(CHUNKS), dma(CHUNKS), dma(CHUNKS), dma(CHUNKS), dma(CHUNKS), dma(CHUNKS), dma(3), dma(3),
        ],
        compiler_params=pltpu.CompilerParams(collective_id=0, has_side_effects=True, vmem_limit_bytes=60 << 20),
        cost_estimate=pl.CostEstimate(flops=2 * length * D * (cols + R), bytes_accessed=16 << 20, transcendentals=0),
    )(tokens, key_weight, u_factor.T, v_factor.T)


def attention_kernel(heads, q_ref, k_ref, u_ref, v_ref, sums_ref, update_ref):
    step = pl.program_id(0)
    length = q_ref.shape[0]
    tile = 256
    scale = 1.0 / math.sqrt(HD)
    twice = scale * math.log2(math.e)

    @pl.when(step == 0)
    def _():
        sums_ref[...] = jnp.zeros_like(sums_ref)

    def parts(value):
        high = value.astype(BF)
        return high, (value - high.astype(F32)).astype(BF)

    u_high, u_rest = parts(u_ref[...])
    v_high, v_rest = parts(v_ref[...])
    product = dot(jnp.concatenate([u_high, u_rest, u_high], axis=1), jnp.concatenate([v_high, v_high, v_rest], axis=1), ((1,), (1,)))
    update_ref[...] = math.sqrt(D * KD / R) * product

    keep = lax.broadcasted_iota(jnp.int32, (tile, tile), 0) <= lax.broadcasted_iota(jnp.int32, (tile, tile), 1)
    for head in range(heads):
        for start in range(0, length, tile):
            q = q_ref[start : start + tile, head * HD : (head + 1) * HD]
            for p in range(2):
                last = dot(k_ref[p, start : start + tile, :], q, ((1,), (1,)))
                last = jnp.where(keep, last, -1e30)
                top = jnp.max(last, axis=0, keepdims=True)
                if start > 0:
                    before = dot(k_ref[p, :start, :], q, ((1,), (1,)))
                    top = jnp.maximum(top, jnp.max(before, axis=0, keepdims=True))
                total = jnp.sum(jnp.exp2((last - top) * twice), axis=0, keepdims=True)
                if start > 0:
                    total += jnp.sum(jnp.exp2((before - top) * twice), axis=0, keepdims=True)
                sums_ref[p : p + 1, start : start + tile] += top * scale + jnp.log(total)


def attend(query_rows, keys, q_u, q_v):
    length, width = query_rows.shape
    rows = q_u.shape[0]
    steps = 8
    heads = width // HD // steps
    return pl.pallas_call(
        functools.partial(attention_kernel, heads),
        grid=(steps,),
        out_shape=(jax.ShapeDtypeStruct((8, length), F32), jax.ShapeDtypeStruct((rows, KD), F32)),
        in_specs=[
            pl.BlockSpec((length, heads * HD), lambda i: (0, i)),
            pl.BlockSpec((2, length, HD), lambda i: (0, 0, i * heads // GROUP)),
            pl.BlockSpec((rows // steps, R), lambda i: (i, 0)),
            pl.BlockSpec((KD, R), lambda i: (0, 0)),
        ],
        out_specs=(pl.BlockSpec((8, length), lambda i: (0, 0)), pl.BlockSpec((rows // steps, KD), lambda i: (i, 0))),
        compiler_params=pltpu.CompilerParams(dimension_semantics=("arbitrary",), vmem_limit_bytes=60 << 20),
    )(query_rows, keys, q_u, q_v)


def loss_kernel(nf, ns, divisor, sums_ref, out_ref, over_f, over_s, f_send, f_recv, s_send, s_recv):
    f = lax.axis_index("fsdp")
    s = lax.axis_index("seq")
    barrier = pltpu.get_barrier_semaphore()

    @pl.loop(1, nf)
    def _(d):
        pl.semaphore_signal(barrier, inc=1, device_id=(lax.rem(f + d, nf), s), device_id_type=MESH)

    @pl.loop(1, ns)
    def _(d):
        pl.semaphore_signal(barrier, inc=1, device_id=(f, lax.rem(s + d, ns)), device_id_type=MESH)

    length = sums_ref.shape[1]
    over_s[s] = sum(sums_ref[:, at : at + 128] for at in range(0, length, 128))
    pl.semaphore_wait(barrier, nf - 1 + ns - 1)

    def copy_s(owner, d):
        return pltpu.make_async_remote_copy(src_ref=over_s.at[owner], dst_ref=over_s.at[owner], send_sem=s_send.at[d],
                                            recv_sem=s_recv.at[d], device_id=(f, lax.rem(s + d, ns)), device_id_type=MESH)

    def copy_f(owner, d):
        return pltpu.make_async_remote_copy(src_ref=over_f.at[owner], dst_ref=over_f.at[owner], send_sem=f_send.at[d],
                                            recv_sem=f_recv.at[d], device_id=(lax.rem(f + d, nf), s), device_id_type=MESH)

    @pl.loop(1, ns)
    def _(d):
        copy_s(s, d).start()

    @pl.loop(1, ns)
    def _(d):
        copy_s(lax.rem(s + ns - d, ns), d).wait_recv()

    over_f[f] = jnp.sum(over_s[...], axis=0)

    @pl.loop(1, nf)
    def _(d):
        copy_f(f, d).start()

    @pl.loop(1, nf)
    def _(d):
        copy_f(lax.rem(f + nf - d, nf), d).wait_recv()

    whole = jnp.sum(over_f[...], axis=0)
    out_ref[...] = jnp.broadcast_to(jnp.sum(whole, axis=1, keepdims=True) * (1.0 / divisor), out_ref.shape)

    @pl.loop(1, ns)
    def _(d):
        copy_s(s, d).wait_send()

    @pl.loop(1, nf)
    def _(d):
        copy_f(f, d).wait_send()


def total_loss(nf, ns, sums, divisor):
    dma = lambda n: pltpu.SemaphoreType.DMA((n,))
    return pl.pallas_call(
        functools.partial(loss_kernel, nf, ns, divisor),
        out_shape=jax.ShapeDtypeStruct((8, 128), F32),
        in_specs=[VMEM],
        out_specs=VMEM,
        scratch_shapes=[pltpu.VMEM((nf, 8, 128), F32), pltpu.VMEM((ns, 8, 128), F32), dma(nf), dma(nf), dma(ns), dma(ns)],
        compiler_params=pltpu.CompilerParams(collective_id=1, has_side_effects=True),
    )(sums)


def solution(mesh):
    nf, ns = mesh.shape["fsdp"], mesh.shape["seq"]

    def local(tokens, queries, key_weight, u_factor, v_factor):
        length = tokens.shape[1] * ns
        keys, q_u, q_v = compute_keys(nf, ns, tokens, key_weight, u_factor, v_factor)
        sums, update = attend(queries[0], keys, q_u, q_v)
        losses = total_loss(nf, ns, sums, float(nf * length * HQ))
        return update, losses[:2, 0]

    in_specs = (
        P("fsdp", "seq", None),
        P("fsdp", None, "seq"),
        P("fsdp", "seq"),
        P("fsdp", None),
        P(),
    )
    out_specs = (P("fsdp", None), P())
    return jax.shard_map(local, mesh=mesh, in_specs=in_specs, out_specs=out_specs, check_vma=False)
```
